128 devices in a mesh: fsdp: 16 (over z_hi, y, core), mp: 8 (over x, z_lo).
Axes of the slice: x: 4, y: 4, z: 4 (z_hi: 2, z_lo: 2; z = z_hi * 2 + z_lo), core: 2. Of those that a mesh axis runs over, the one named last changes fastest.
Arguments:
- tokens: bfloat16 [512, 16384], P('mp', 'fsdp'), may hold values from -6 to 6
- frozen_weights: bfloat16 [3, 26624, 16384], P(None, ('fsdp', 'mp')), may hold values from -0.046875 to 0.046875
- hidden_adapter_factor: bfloat16 [3, 26624, 64], P(None, ('fsdp', 'mp')), may hold values from -0.75 to 0.75
- feature_adapter_factor: bfloat16 [3, 64, 16384], P(None, None, ('fsdp', 'mp')), may hold values from -0.046875 to 0.046875
Outputs:
- block_out: bfloat16 [512, 16384], P('mp', 'fsdp')
The draws below stay inside these ranges and needn't reach their ends.
All inputs are finite; a program needn't handle non-finite values.
Results may differ from the reference program's by a relative error of at most 0.038.
Values may be sent and summed in bfloat16 or wider, within the bound.
No kernel may reach another device: no remote copies, remote signals or barrier semaphores. Data moves between devices by JAX's collectives and lax.ppermute only.
A program may use at most 192 MiB of HBM per device.

```python
import jax
import jax.numpy as jnp
from jax import lax

MODEL_WIDTH = 16384
HIDDEN_HALF = 26624
ADAPTER_RANK = 64
TOKENS = 512
N_FSDP = 16


def level_of(stream_key, dims, cuts, smallest, largest):
    loudness = 1.0
    for dim, shards_of in cuts:
        draws = jax.random.uniform(jax.random.fold_in(jax.random.fold_in(stream_key, 6), dim), (shards_of,), jnp.float32, smallest / len(cuts), largest / len(cuts))
        loudness = loudness * jnp.repeat(jnp.exp(draws), dims[dim] // shards_of).reshape((-1,) + (1,) * (len(dims) - 1 - dim))
    return loudness


def gaussian(own_key, dims, width, limit, cuts=(), kind=jnp.bfloat16):
    values = jax.random.normal(own_key, dims, jnp.float32) * width
    if len(cuts) > 0:
        values = level_of(own_key, dims, cuts, -0.22, 0.18) * values
    return jnp.clip(values, min=-limit, max=limit).astype(kind)


def setup_inputs(seed: int = 0) -> dict:
    keys = jax.random.split(jax.random.key(seed), 5)
    tokens = gaussian(keys[0], (TOKENS, MODEL_WIDTH), 1.0, 6.0, ((0, 8), (1, 16)))
    frozen_weights = gaussian(keys[1], (3, HIDDEN_HALF, MODEL_WIDTH), MODEL_WIDTH ** -0.5, 0.046875, ((1, 128),))
    hidden_adapter_factor = gaussian(keys[2], (3, HIDDEN_HALF, ADAPTER_RANK), ADAPTER_RANK ** -0.5, 0.75, ((1, 128),))
    feature_adapter_factor = gaussian(keys[3], (3, ADAPTER_RANK, MODEL_WIDTH), MODEL_WIDTH ** -0.5, 0.046875, ((2, 128),))
    return dict(tokens=tokens, frozen_weights=frozen_weights, hidden_adapter_factor=hidden_adapter_factor, feature_adapter_factor=feature_adapter_factor)


def combined_columns(frozen_weights, hidden_adapter_factor, feature_adapter_factor, projection_index, starting_column, column_count):
    base_block = frozen_weights[projection_index][:, starting_column:starting_column + column_count].astype(jnp.float32)
    feature_factor_block = feature_adapter_factor[projection_index][:, starting_column:starting_column + column_count]
    weight_update = jnp.dot(hidden_adapter_factor[projection_index], feature_factor_block, preferred_element_type=jnp.float32)
    return (base_block + weight_update).astype(jnp.bfloat16)


def rounded_update_part(input_tokens, weight_block):
    product = lax.dot_general(input_tokens, weight_block, (((1,), (1,)), ((), ())), preferred_element_type=jnp.float32)
    return lax.optimization_barrier(product.astype(jnp.bfloat16)).astype(jnp.float32)


def reference(tokens, frozen_weights, hidden_adapter_factor, feature_adapter_factor):
    column_width = MODEL_WIDTH // N_FSDP
    gate_total = jnp.zeros((TOKENS, HIDDEN_HALF), jnp.float32)
    up_total = jnp.zeros((TOKENS, HIDDEN_HALF), jnp.float32)
    for block_index in range(N_FSDP):
        starting_column = block_index * column_width
        input_tokens = tokens[:, starting_column:starting_column + column_width]
        gate_total = gate_total + rounded_update_part(input_tokens, combined_columns(frozen_weights, hidden_adapter_factor, feature_adapter_factor, 0, starting_column, column_width))
        up_total = up_total + rounded_update_part(input_tokens, combined_columns(frozen_weights, hidden_adapter_factor, feature_adapter_factor, 1, starting_column, column_width))
    hidden = (jax.nn.silu(gate_total) * up_total).astype(jnp.bfloat16)
    outputs = []
    for block_index in range(N_FSDP):
        starting_column = block_index * column_width
        down_weight_block = combined_columns(frozen_weights, hidden_adapter_factor, feature_adapter_factor, 2, starting_column, column_width)
        outputs.append(jnp.dot(hidden, down_weight_block, preferred_element_type=jnp.float32).astype(jnp.bfloat16))
    return jnp.concatenate(outputs, axis=1)
```

```python
import jax
import jax.numpy as jnp
from jax import lax
from jax.experimental import pallas as pl
from jax.experimental.pallas import tpu as pltpu
from jax.sharding import Mesh, PartitionSpec as P

NAMES = ("zh", "y", "c", "x", "zl")
SIZES = (2, 4, 2, 4, 2)
ROWS = 208
TOK = 512
GROUP = 64
BLOCK = 1024
NB = 8
RANK = 64
WIDE = BLOCK + 128
PART = WIDE // 3
ORDERS = ((1, 2, 0), (2, 0, 1), (0, 1, 2))
VMEM = 60 * 1024 * 1024


def pairs(move):
    out = []
    for i in range(128):
        zh, y, c, x, zl = i // 64, i // 16 % 4, i // 8 % 2, i // 2 % 4, i % 2
        x, y, z, c = move(x, y, 2 * zh + zl, c)
        out.append((i, (((z // 2 * 4 + y) * 2 + c) * 4 + x) * 2 + z % 2))
    return out


def axis_pairs(axis, first):
    def move(x, y, z, c):
        q = [x, y, z]
        q[axis] ^= 1 if (c == 0) == first else 3
        return (*q, c)

    return pairs(move)


FIRST = [axis_pairs(a, True) for a in range(3)]
SECOND = [axis_pairs(a, False) for a in range(3)]
CORES = pairs(lambda x, y, z, c: (x, y, z, 1 - c))


def send(value, table):
    return lax.ppermute(value, NAMES, table)


def gather_part(value, order):
    value = value[None]
    for stage, axis in enumerate(order):
        mine = jnp.stack([value, send(value, FIRST[axis])])
        theirs = send(mine, SECOND[axis])
        if stage < 2:
            value = jnp.concatenate([mine, theirs]).reshape(-1, *value.shape[1:])
    return mine, theirs


def scatter_part(keep, away, order):
    for stage, axis in enumerate(order[::-1]):
        if stage > 0:
            keep, away = total.reshape(2, 2, -1, GROUP, PART)
        pair = keep + send(away, SECOND[axis])
        total = pair[0] + send(pair[1], FIRST[axis])
    return total.reshape(GROUP, PART)


def coordinate(place, k, core):
    return place ^ jnp.where(core == 0, (0, 1, 3, 2)[k], (0, 3, 1, 2)[k])


def relative(place, there, core):
    e = place ^ there
    zero = jnp.where(e == 1, 1, jnp.where(e == 3, 2, jnp.where(e == 2, 3, 0)))
    one = jnp.where(e == 3, 1, jnp.where(e == 1, 2, jnp.where(e == 2, 3, 0)))
    return jnp.where(core == 0, zero, one)


def split_kernel(place, w, out):
    out[...] = w[0]


def split(place, weights, k):
    return pl.pallas_call(
        split_kernel,
        out_shape=jax.ShapeDtypeStruct((ROWS, NB * BLOCK), jnp.bfloat16),
        grid_spec=pltpu.PrefetchScalarGridSpec(
            num_scalar_prefetch=1,
            grid=(NB,),
            in_specs=[pl.BlockSpec((1, ROWS, BLOCK), lambda j, s: (k, 0, 2 * j + 1 - s[0]))],
            out_specs=pl.BlockSpec((ROWS, BLOCK), lambda j, s: (0, j)),
        ),
        compiler_params=pltpu.CompilerParams(vmem_limit_bytes=VMEM),
        name="split",
    )(place, weights)


def dot_t(a, b):
    return lax.dot_general(a, b, (((1,), (1,)), ((), ())), preferred_element_type=jnp.float32)


def up_kernel(place, w, wg, wu, a_mine, a_other, *refs):
    blocks, (out, xs, acc, tacc, sems) = refs[:6], refs[6:]
    j = pl.program_id(0)
    core = place[0]

    @pl.when(j == 0)
    def _():
        at = [[coordinate(place[1 + a], k, core) for k in range(4)] for a in range(3)]
        for third in range(4):
            for second in range(4):
                for first in range(4):
                    for part, order in enumerate(ORDERS):
                        q = [None] * 3
                        q[order[0]], q[order[1]], q[order[2]] = (
                            at[order[0]][first], at[order[1]][second], at[order[2]][third],
                        )
                        x, y, z = q
                        block = (z // 2) * 4 + y
                        group = x * 2 + (z & 1)
                        pltpu.make_async_copy(
                            blocks[2 * part + third // 2].at[third % 2, second * 4 + first],
                            xs.at[
                                block,
                                pl.ds(pl.multiple_of(group * GROUP, GROUP), GROUP),
                                pl.ds(part * PART, PART),
                            ],
                            sems.at[block],
                        ).start()
        acc[...] = jnp.zeros_like(acc)
        tacc[...] = jnp.zeros_like(tacc)

    pltpu.make_async_copy(xs.at[j], xs.at[j], sems.at[j]).wait()
    x = xs[j, :, :BLOCK]
    acc[0] += dot_t(x, w[0])
    acc[1] += dot_t(x, w[1])
    acc[2] += dot_t(x, wg[...])
    acc[3] += dot_t(x, wu[...])
    tacc[...] += xs[j, :, BLOCK:].astype(jnp.float32)

    @pl.when(j == NB - 1)
    def _():
        t = tacc[...].astype(jnp.bfloat16)
        for side, a in enumerate((a_mine, a_other)):
            for k in range(2):
                low = dot_t(t[:, k * RANK : (k + 1) * RANK], a[k])
                out[side, k] = (acc[2 * side + k] + low).astype(jnp.bfloat16)


def up(place, weights, wg, wu, a_mine, a_other, blocks):
    any_spec = pl.BlockSpec(memory_space=pl.ANY)
    a_spec = pl.BlockSpec((3, ROWS, RANK), lambda j, s: (0, 0, 0))
    return pl.pallas_call(
        up_kernel,
        out_shape=jax.ShapeDtypeStruct((2, 2, TOK, ROWS), jnp.bfloat16),
        grid_spec=pltpu.PrefetchScalarGridSpec(
            num_scalar_prefetch=1,
            grid=(NB,),
            in_specs=[
                pl.BlockSpec((2, ROWS, BLOCK), lambda j, s: (0, 0, 2 * j + s[0])),
                pl.BlockSpec((ROWS, BLOCK), lambda j, s: (0, j)),
                pl.BlockSpec((ROWS, BLOCK), lambda j, s: (0, j)),
                a_spec,
                a_spec,
                *[any_spec] * 6,
            ],
            out_specs=pl.BlockSpec((2, 2, TOK, ROWS), lambda j, s: (0, 0, 0, 0)),
            scratch_shapes=[
                pltpu.VMEM((NB, TOK, WIDE), jnp.bfloat16),
                pltpu.VMEM((4, TOK, ROWS), jnp.float32),
                pltpu.VMEM((TOK, 128), jnp.float32),
                pltpu.SemaphoreType.DMA((NB,)),
            ],
        ),
        compiler_params=pltpu.CompilerParams(vmem_limit_bytes=VMEM),
        name="up",
    )(place, weights, wg, wu, a_mine, a_other, *blocks)


def down_kernel(place, mine, other, w, wd, a_mine, a_other, *refs):
    outs, (hidden, ob, sems) = refs[:6], refs[6:]
    j = pl.program_id(0)
    slot = lax.rem(j, 2)
    core = place[0]

    def drain(s):
        pltpu.make_async_copy(ob.at[s], ob.at[s], sems.at[s]).wait()

    @pl.when(j == 0)
    def _():
        for side in range(2):
            f32 = jnp.float32
            gate = mine[side, 0].astype(f32) + other[1 - side, 0].astype(f32)
            upper = mine[side, 1].astype(f32) + other[1 - side, 1].astype(f32)
            hidden[side] = (gate / (1.0 + jnp.exp(-gate)) * upper).astype(jnp.bfloat16)
        low = jnp.dot(hidden[0], a_mine[2], preferred_element_type=jnp.float32)
        low += jnp.dot(hidden[1], a_other[2], preferred_element_type=jnp.float32)
        for s in range(2):
            ob[s, :, BLOCK:] = jnp.concatenate([low, jnp.zeros_like(low)], axis=1).astype(jnp.bfloat16)

    @pl.when(j >= 2)
    def _():
        drain(slot)

    value = jnp.dot(hidden[0], w[0], preferred_element_type=jnp.float32)
    value += jnp.dot(hidden[1], wd[...], preferred_element_type=jnp.float32)
    ob[slot, :, :BLOCK] = value.astype(jnp.bfloat16)

    zh, y = j // 4, lax.rem(j, 4)
    rel_y = relative(place[2], y, core)
    for group in range(8):
        x, zl = group // 2, group % 2
        rel = (relative(place[1], x, core), rel_y, relative(place[3], 2 * zh + zl, core))
        for part, order in enumerate(ORDERS):
            first, second, third = (rel[a] for a in order)
            source = ob.at[slot, pl.ds(group * GROUP, GROUP), pl.ds(part * PART, PART)]
            for half in range(2):

                @pl.when(third // 2 == half)
                def _():
                    pltpu.make_async_copy(
                        source,
                        outs[2 * part + half].at[third % 2, second * 4 + first],
                        sems.at[slot],
                    ).start()

    @pl.when(j == NB - 1)
    def _():
        drain(0)
        drain(1)


def down(place, mine, other, weights, wd, a_mine, a_other):
    part_spec = pl.BlockSpec((2, 2, TOK, ROWS), lambda j, s: (0, 0, 0, 0))
    a_spec = pl.BlockSpec((3, ROWS, RANK), lambda j, s: (0, 0, 0))
    return pl.pallas_call(
        down_kernel,
        out_shape=[jax.ShapeDtypeStruct((2, 16, GROUP, PART), jnp.bfloat16)] * 6,
        grid_spec=pltpu.PrefetchScalarGridSpec(
            num_scalar_prefetch=1,
            grid=(NB,),
            in_specs=[
                part_spec,
                part_spec,
                pl.BlockSpec((1, ROWS, BLOCK), lambda j, s: (2, 0, 2 * j + s[0])),
                pl.BlockSpec((ROWS, BLOCK), lambda j, s: (0, j)),
                a_spec,
                a_spec,
            ],
            out_specs=[pl.BlockSpec(memory_space=pl.ANY)] * 6,
            scratch_shapes=[
                pltpu.VMEM((2, TOK, ROWS), jnp.bfloat16),
                pltpu.VMEM((2, TOK, WIDE), jnp.bfloat16),
                pltpu.SemaphoreType.DMA((2,)),
            ],
        ),
        compiler_params=pltpu.CompilerParams(vmem_limit_bytes=VMEM),
        name="down",
    )(place, mine, other, weights, wd, a_mine, a_other)


def group_features(factor, x, zl):
    flat = factor.reshape(3 * RANK, 128)
    across = []
    for step in range(4):
        got = flat if step == 0 else send(
            flat, pairs(lambda x, y, z, c: ((x + step) % 4, y, z, c))
        )
        across.append(got)
    wide = jnp.concatenate(across, axis=0)
    other = send(wide, pairs(lambda x, y, z, c: (x, y, z ^ 1, c)))
    out = jnp.zeros((3 * RANK, BLOCK), factor.dtype)
    for step in range(4):
        column = ((x - step) % 4) * 2
        rows = slice(step * 3 * RANK, (step + 1) * 3 * RANK)
        out = lax.dynamic_update_slice(out, wide[rows], (0, (column + zl) * 128))
        out = lax.dynamic_update_slice(out, other[rows], (0, (column + 1 - zl) * 128))
    return out


def per_device(tokens, frozen_weights, hidden_adapter_factor, feature_adapter_factor):
    zh, y, core, x, zl = (lax.axis_index(n) for n in NAMES)
    place = jnp.stack([core, x, y, 2 * zh + zl]).astype(jnp.int32)
    factor = group_features(feature_adapter_factor, x, zl)
    low = dot_t(tokens, factor[: 2 * RANK]).astype(jnp.bfloat16)
    parts = (
        tokens[:, :PART],
        tokens[:, PART : 2 * PART],
        jnp.concatenate([tokens[:, 2 * PART :], low], axis=1),
    )
    others = [send(split(place, frozen_weights, k), CORES) for k in range(3)]
    a_other = send(hidden_adapter_factor, CORES)
    blocks = [b for p, o in zip(parts, ORDERS) for b in gather_part(p, o)]
    mine = up(place, frozen_weights, others[0], others[1], hidden_adapter_factor, a_other, blocks)
    theirs = send(mine, CORES)
    sums = down(place, mine, theirs, frozen_weights, others[2], hidden_adapter_factor, a_other)
    left, middle, right = (
        scatter_part(sums[2 * p], sums[2 * p + 1], ORDERS[p]) for p in range(3)
    )
    last = BLOCK - 2 * PART
    plain = jnp.concatenate([left, middle, right[:, :last]], axis=1).astype(jnp.float32)
    extra = jnp.dot(
        right[:, last : last + RANK], factor[2 * RANK :], preferred_element_type=jnp.float32
    )
    return (plain + extra).astype(jnp.bfloat16)


def solution(mesh):
    fine = Mesh(mesh.devices.reshape(SIZES), NAMES)
    units = ("zh", "y", "c", "x", "zl")
    return jax.shard_map(
        per_device,
        mesh=fine,
        in_specs=(
            P(("x", "zl"), ("zh", "y", "c")),
            P(None, units, None),
            P(None, units, None),
            P(None, None, units),
        ),
        out_specs=P(("x", "zl"), ("zh", "y", "c")),
        check_vma=False,
    )
```

```python
import jax
import jax.numpy as jnp
from jax import lax
from jax.experimental import pallas as pl
from jax.experimental.pallas import tpu as pltpu
from jax.sharding import Mesh, PartitionSpec as P

NAMES = ("zh", "y", "c", "x", "zl")
SIZES = (2, 4, 2, 4, 2)
ROWS = 208
TOK = 512
GROUP = 64
BLOCK = 1024
NB = 8
RANK = 64
WIDE = BLOCK + 128
PART = WIDE // 3
SYNC = True
RSYNC = True
DIRECT = 0
ORDERS = ((1, 2, 0), (2, 0, 1), (0, 1, 2))
VMEM = 60 * 1024 * 1024


def pairs(move):
    out = []
    for i in range(128):
        zh, y, c, x, zl = i // 64, i // 16 % 4, i // 8 % 2, i // 2 % 4, i % 2
        x, y, z, c = move(x, y, 2 * zh + zl, c)
        out.append((i, (((z // 2 * 4 + y) * 2 + c) * 4 + x) * 2 + z % 2))
    return out


def axis_pairs(axis, first):
    def move(x, y, z, c):
        q = [x, y, z]
        q[axis] ^= 1 if (c == 0) == first else 3
        return (*q, c)

    return pairs(move)


FIRST = [axis_pairs(a, True) for a in range(3)]
SECOND = [axis_pairs(a, False) for a in range(3)]


def across_pairs(axis):
    def move(x, y, z, c):
        q = [x, y, z]
        q[axis] ^= 2
        return (*q, c)

    return pairs(move)


ACROSS = [across_pairs(a) for a in range(3)]
CORES = pairs(lambda x, y, z, c: (x, y, z, 1 - c))


def send(value, table):
    return lax.ppermute(value, NAMES, table)


def gather(values):
    for stage in range(3):
        axes = [order[stage] for order in ORDERS]
        if stage < DIRECT:
            got = [
                [v] + [send(v, t[a]) for t in (FIRST, SECOND, ACROSS)]
                for v, a in zip(values, axes)
            ]
            values = [jnp.stack(g).reshape(-1, *g[0].shape[1:]) for g in got]
            if SYNC: values = lax.optimization_barrier(values)
            continue
        mine = [jnp.stack([v, send(v, FIRST[a])]) for v, a in zip(values, axes)]
        if False: mine = lax.optimization_barrier(mine)
        theirs = [send(v, SECOND[a]) for v, a in zip(mine, axes)]
        if stage < 2:
            values = [
                jnp.concatenate(p).reshape(-1, *v.shape[1:])
                for p, v in zip(zip(mine, theirs), values)
            ]
            if SYNC: values = lax.optimization_barrier(values)
    return [b for p in zip(mine, theirs) for b in p]


def scatter(keep, away):
    for stage in range(2, -1, -1):
        axes = [order[stage] for order in ORDERS]
        if stage < 2:
            keep, away = zip(*(t.reshape(2, 2, -1, GROUP, PART) for t in totals))
        if stage < DIRECT:
            totals = []
            for k, w, a in zip(keep, away, axes):
                got = [send(k[1], FIRST[a]), send(w[0], SECOND[a]), send(w[1], ACROSS[a])]
                totals.append(sum((g.astype(jnp.float32) for g in got), k[0].astype(jnp.float32)).astype(jnp.bfloat16))
            continue
        pairs_ = [k + send(w, SECOND[a]) for k, w, a in zip(keep, away, axes)]
        if False: pairs_ = lax.optimization_barrier(pairs_)
        totals = [p[0] + send(p[1], FIRST[a]) for p, a in zip(pairs_, axes)]
        if RSYNC and stage > 0: totals = lax.optimization_barrier(totals)
    return [t.reshape(GROUP, PART) for t in totals]


def coordinate(place, k, core):
    return place ^ jnp.where(core == 0, (0, 1, 3, 2)[k], (0, 3, 1, 2)[k])


def relative(place, there, core):
    e = place ^ there
    zero = jnp.where(e == 1, 1, jnp.where(e == 3, 2, jnp.where(e == 2, 3, 0)))
    one = jnp.where(e == 3, 1, jnp.where(e == 1, 2, jnp.where(e == 2, 3, 0)))
    return jnp.where(core == 0, zero, one)


def dot_t(a, b):
    return lax.dot_general(a, b, (((1,), (1,)), ((), ())), preferred_element_type=jnp.float32)


def copy(source, target, sem):
    pltpu.make_async_copy(source, target, sem).start()


def await_all(target, sem):
    pltpu.make_async_copy(target, target, sem).wait()


def up_kernel(place, w, wo, a_mine, a_other, *refs):
    blocks, (out, factor, ws, xs, acc, wsems, xsems, bsems, fsem) = refs[:6], refs[6:]
    core = place[0]
    at = [[coordinate(place[1 + a], k, core) for k in range(4)] for a in range(3)]
    near = place[3] // 2
    steps = [(near if j < 4 else 1 - near, j % 4) for j in range(NB)]

    def weights(zh, ky):
        columns = pl.ds(pl.multiple_of((2 * (4 * zh + at[1][ky]) + core) * BLOCK, BLOCK), BLOCK)
        block = 4 * zh + ky
        for side, source in enumerate((w, wo)):
            for k in range(2):
                rows = pl.ds((2 * side + k) * ROWS, ROWS)
                copy(source.at[k, :, columns], ws.at[block, rows], wsems.at[block])

    weights(*steps[0])
    left, middle, right = (blocks[i : i + 2] for i in (0, 2, 4))
    for kz in range(4):
        zh, zl = at[2][kz] // 2, at[2][kz] & 1
        block = pl.ds(4 * zh, 4)
        last = BLOCK - 2 * PART
        copy(
            right[kz // 2].at[kz % 2, :, :, :, pl.ds(0, last)],
            xs.at[block, :, zl, :, pl.ds(2 * PART, last)],
            xsems.at[zh],
        )
        for k in range(4):
            copy(
                left[k // 2].at[k % 2, kz, :, :, pl.ds(0, PART)],
                xs.at[block, k, zl, :, pl.ds(0, PART)],
                xsems.at[zh],
            )
            copy(
                middle[k // 2].at[k % 2, :, kz],
                xs.at[4 * zh + k, :, zl, :, pl.ds(PART, PART)],
                xsems.at[zh],
            )
            columns = pl.ds(pl.multiple_of((2 * at[0][k] + zl) * 128, 128), 128)
            for part in range(2):
                copy(
                    right[kz // 2].at[kz % 2, :, k, :, pl.ds(last + part * 128, 128)],
                    ws.at[block, pl.ds(4 * ROWS + part * RANK, RANK), columns],
                    bsems.at[zh],
                )
    for k in range(4):
        for kz in (0, 1 + core):
            zl = place[3] & 1 if isinstance(kz, int) else 1 - (place[3] & 1)
            columns = pl.ds(pl.multiple_of((2 * at[0][k] + zl) * 128, 128), 128)
            copy(left[k // 2].at[k % 2, kz, 0, :, pl.ds(PART, 128)], factor.at[:, columns], fsem)
    for j in range(1, NB):
        weights(*steps[j])

    for j, (zh, ky) in enumerate(steps):
        block = 4 * zh + ky
        if j % 4 == 0:
            await_all(xs.at[pl.ds(4 * zh, 4)], xsems.at[zh])
            await_all(ws.at[pl.ds(4 * zh, 4), pl.ds(4 * ROWS, 2 * RANK)], bsems.at[zh])
        await_all(ws.at[block, pl.ds(0, 4 * ROWS)], wsems.at[block])
        product = dot_t(ws[block], xs[block].reshape(TOK, BLOCK))
        if j == 0:
            acc[...] = product
        else:
            acc[...] += product
    t = acc[4 * ROWS :].astype(jnp.bfloat16)
    for side, a in enumerate((a_mine, a_other)):
        for k in range(2):
            low = jnp.dot(a[k], t[k * RANK : (k + 1) * RANK], preferred_element_type=jnp.float32)
            rows = (2 * side + k) * ROWS
            out[side, k] = (acc[rows : rows + ROWS] + low).astype(jnp.bfloat16)
    await_all(factor, fsem)


ANY = pl.BlockSpec(memory_space=pl.ANY)
ON_CHIP = pl.BlockSpec(memory_space=pltpu.VMEM)
SCALARS = pl.BlockSpec(memory_space=pltpu.SMEM)


def up(place, weights, others, a_mine, a_other, blocks):
    return pl.pallas_call(
        up_kernel,
        out_shape=[
            jax.ShapeDtypeStruct((2, 2, ROWS, TOK), jnp.bfloat16),
            jax.ShapeDtypeStruct((RANK, BLOCK), jnp.bfloat16),
        ],
        in_specs=[SCALARS, ANY, ANY, ON_CHIP, ON_CHIP, *[ANY] * 6],
        out_specs=[ON_CHIP, ON_CHIP],
        scratch_shapes=[
            pltpu.VMEM((NB, 4 * ROWS + 2 * RANK, BLOCK), jnp.bfloat16),
            pltpu.VMEM((NB, 4, 2, GROUP, BLOCK), jnp.bfloat16),
            pltpu.VMEM((4 * ROWS + 2 * RANK, TOK), jnp.float32),
            pltpu.SemaphoreType.DMA((NB,)),
            pltpu.SemaphoreType.DMA((2,)),
            pltpu.SemaphoreType.DMA((2,)),
            pltpu.SemaphoreType.DMA,
        ],
        compiler_params=pltpu.CompilerParams(vmem_limit_bytes=VMEM),
        name="up",
    )(place, weights, others, a_mine, a_other, *blocks)


def down_kernel(place, mine, other, w, wo, a_mine, a_other, *refs):
    outs, (ws, hidden, ob, wsems, osems) = refs[:6], refs[6:]
    core = place[0]
    for j in range(NB):
        there = 2 * (4 * (j // 4) + coordinate(place[2], j % 4, core)) + core
        columns = pl.ds(pl.multiple_of(there * BLOCK, BLOCK), BLOCK)
        for side, source in enumerate((w, wo)):
            copy(source.at[2, :, columns], ws.at[j, pl.ds(side * ROWS, ROWS)], wsems.at[j])
    f32 = jnp.float32

    def both(side, k):
        theirs = [other[1 - side, k, :, i * 128 : (i + 1) * 128] for i in (0, 2, 1, 3)]
        return mine[side, k].astype(f32) + jnp.concatenate(theirs, axis=1).astype(f32)

    halves = []
    for side in range(2):
        gate, upper = both(side, 0), both(side, 1)
        halves.append(gate / (1.0 + jnp.exp(-gate)) * upper)
    hidden[...] = jnp.concatenate(halves, axis=0).T.astype(jnp.bfloat16)
    factor = jnp.concatenate([a_mine[2], a_other[2]], axis=0)
    low = jnp.dot(hidden[...], factor, preferred_element_type=f32)
    low = jnp.concatenate([low, jnp.zeros_like(low)], axis=1).astype(jnp.bfloat16)
    rel_z = [relative(place[3], z, core) for z in range(4)]
    left, middle, right = (outs[i : i + 2] for i in (0, 2, 4))
    for j in range(NB):
        zh, ky = j // 4, j % 4
        await_all(ws.at[j], wsems.at[j])
        value = jnp.dot(hidden[...], ws[j], preferred_element_type=f32).astype(jnp.bfloat16)
        ob[j, :, :, :, :BLOCK] = value.reshape(4, 2, GROUP, BLOCK)
        ob[j, :, :, :, BLOCK:] = low.reshape(4, 2, GROUP, 128)
        for zl in range(2):
            kz = rel_z[2 * zh + zl]
            for kx in range(4):
                copy(
                    ob.at[j, kx, zl, :, pl.ds(0, PART)],
                    left[kx // 2].at[kx % 2, kz, ky],
                    osems.at[j],
                )
            copy(
                ob.at[j, :, zl, :, pl.ds(PART, PART)],
                middle[ky // 2].at[ky % 2, :, kz],
                osems.at[j],
            )
            for half in range(2):

                @pl.when(kz // 2 == half)
                def _():
                    copy(
                        ob.at[j, :, zl, :, pl.ds(2 * PART, PART)],
                        right[half].at[kz % 2, ky],
                        osems.at[j],
                    )
    for j in range(NB):
        await_all(ob.at[j], osems.at[j])


def down(place, mine, other, weights, others, a_mine, a_other):
    return pl.pallas_call(
        down_kernel,
        out_shape=[jax.ShapeDtypeStruct((2, 4, 4, GROUP, PART), jnp.bfloat16)] * 6,
        in_specs=[SCALARS, ON_CHIP, ON_CHIP, ANY, ANY, ON_CHIP, ON_CHIP],
        out_specs=[ANY] * 6,
        scratch_shapes=[
            pltpu.VMEM((NB, 2 * ROWS, BLOCK), jnp.bfloat16),
            pltpu.VMEM((TOK, 2 * ROWS), jnp.bfloat16),
            pltpu.VMEM((NB, 4, 2, GROUP, WIDE), jnp.bfloat16),
            *[pltpu.SemaphoreType.DMA((NB,))] * 2,
        ],
        compiler_params=pltpu.CompilerParams(vmem_limit_bytes=VMEM),
        name="down",
    )(place, mine, other, weights, others, a_mine, a_other)


def per_device(tokens, frozen_weights, hidden_adapter_factor, feature_adapter_factor):
    zh, y, core, x, zl = (lax.axis_index(n) for n in NAMES)
    place = jnp.stack([core, x, y, 2 * zh + zl]).astype(jnp.int32)
    others = send(frozen_weights, CORES)
    a_other = send(hidden_adapter_factor, CORES)
    gate_factor, up_factor, down_factor = feature_adapter_factor
    blocks = gather([
        jnp.concatenate([tokens[:, :PART], down_factor], axis=1)[None],
        tokens[None, :, PART : 2 * PART],
        jnp.concatenate([tokens[:, 2 * PART :], gate_factor, up_factor], axis=1)[None],
    ])
    blocks = [v.reshape(2, 4, 4, *v.shape[2:]) for v in blocks]
    mine, factor = up(place, frozen_weights, others, hidden_adapter_factor, a_other, blocks)
    theirs = send(mine, CORES)
    sums = down(place, mine, theirs, frozen_weights, others, hidden_adapter_factor, a_other)
    left, middle, right = scatter(
        [v.reshape(2, 16, GROUP, PART) for v in sums[::2]],
        [v.reshape(2, 16, GROUP, PART) for v in sums[1::2]],
    )
    last = BLOCK - 2 * PART
    plain = jnp.concatenate([left, middle, right[:, :last]], axis=1).astype(jnp.float32)
    extra = jnp.dot(
        right[:, last : last + RANK], factor, preferred_element_type=jnp.float32
    )
    return (plain + extra).astype(jnp.bfloat16)


def solution(mesh):
    fine = Mesh(mesh.devices.reshape(SIZES), NAMES)
    units = ("zh", "y", "c", "x", "zl")
    return jax.shard_map(
        per_device,
        mesh=fine,
        in_specs=(
            P(("x", "zl"), ("zh", "y", "c")),
            P(None, units, None),
            P(None, units, None),
            P(None, None, units),
        ),
        out_specs=P(("x", "zl"), ("zh", "y", "c")),
        check_vma=False,
    )
```

```python
import jax
import jax.numpy as jnp
from jax import lax
from jax.experimental import pallas as pl
from jax.experimental.pallas import tpu as pltpu
from jax.sharding import Mesh, PartitionSpec as P

NAMES = ("zh", "y", "c", "x", "zl")
SIZES = (2, 4, 2, 4, 2)
ROWS = 208
TOK = 512
GROUP = 64
BLOCK = 1024
NB = 8
RANK = 64
WIDE = BLOCK + 128
PART = WIDE // 3
ORDERS = ((1, 2, 0), (2, 0, 1), (0, 1, 2))
VMEM = 60 * 1024 * 1024


def pairs(move):
    out = []
    for i in range(128):
        zh, y, c, x, zl = i // 64, i // 16 % 4, i // 8 % 2, i // 2 % 4, i % 2
        x, y, z, c = move(x, y, 2 * zh + zl, c)
        out.append((i, (((z // 2 * 4 + y) * 2 + c) * 4 + x) * 2 + z % 2))
    return out


def axis_pairs(axis, first):
    def move(x, y, z, c):
        q = [x, y, z]
        q[axis] ^= 1 if (c == 0) == first else 3
        return (*q, c)

    return pairs(move)


FIRST = [axis_pairs(a, True) for a in range(3)]
SECOND = [axis_pairs(a, False) for a in range(3)]


CORES = pairs(lambda x, y, z, c: (x, y, z, 1 - c))


def send(value, table):
    return lax.ppermute(value, NAMES, table)


def gather(values, late):
    for stage in range(2):
        axes = [order[stage] for order in ORDERS]
        mine = [jnp.stack([v, send(v, FIRST[a])]) for v, a in zip(values, axes)]
        theirs = [send(v, SECOND[a]) for v, a in zip(mine, axes)]
        values = [
            jnp.concatenate(p).reshape(-1, *v.shape[1:])
            for p, v in zip(zip(mine, theirs), values)
        ]
        if stage == 1:
            values[1], late = lax.optimization_barrier((values[1], late))
    out = []
    for v, order in zip(values, ORDERS):
        near = send(v, FIRST[order[2]])
        out += [v, near, send(v, SECOND[order[2]]), send(near, SECOND[order[2]])]
    return out, late


def scatter(sums):
    totals = []
    for part, order in enumerate(ORDERS):
        blocks = [v.reshape(16, GROUP, PART) for v in sums[4 * part : 4 * part + 4]]
        across = blocks[1] + send(blocks[3], SECOND[order[2]])
        second = send(blocks[2], SECOND[order[2]])
        first = send(across, FIRST[order[2]])
        total = sum(v.astype(jnp.float32) for v in (blocks[0], second, first))
        totals.append(total.astype(jnp.bfloat16))
    for stage in (1, 0):
        axes = [order[stage] for order in ORDERS]
        keep, away = zip(*(t.reshape(2, 2, -1, GROUP, PART) for t in totals))
        halves = [k + send(w, SECOND[a]) for k, w, a in zip(keep, away, axes)]
        totals = [p[0] + send(p[1], FIRST[a]) for p, a in zip(halves, axes)]
    return [t.reshape(GROUP, PART) for t in totals]


def coordinate(place, k, core):
    return place ^ jnp.where(core == 0, (0, 1, 3, 2)[k], (0, 3, 1, 2)[k])


def relative(place, there, core):
    e = place ^ there
    zero = jnp.where(e == 1, 1, jnp.where(e == 3, 2, jnp.where(e == 2, 3, 0)))
    one = jnp.where(e == 3, 1, jnp.where(e == 1, 2, jnp.where(e == 2, 3, 0)))
    return jnp.where(core == 0, zero, one)


def dot_t(a, b):
    return lax.dot_general(a, b, (((1,), (1,)), ((), ())), preferred_element_type=jnp.float32)


def copy(source, target, sem):
    pltpu.make_async_copy(source, target, sem).start()


def await_all(target, sem):
    pltpu.make_async_copy(target, target, sem).wait()


def up_kernel(place, w, wo, a_mine, a_other, *refs):
    blocks, (out, factor, ws, xs, acc, wsems, xsems, bsems, fsem) = refs[:12], refs[12:]
    core = place[0]
    at = [[coordinate(place[1 + a], k, core) for k in range(4)] for a in range(3)]
    near = place[3] // 2
    steps = [(near if j < 4 else 1 - near, j % 4) for j in range(NB)]

    def weights(zh, ky):
        columns = pl.ds(pl.multiple_of((2 * (4 * zh + at[1][ky]) + core) * BLOCK, BLOCK), BLOCK)
        block = 4 * zh + ky
        for side, source in enumerate((w, wo)):
            for k in range(2):
                rows = pl.ds((2 * side + k) * ROWS, ROWS)
                copy(source.at[k, :, columns], ws.at[block, rows], wsems.at[block])

    weights(*steps[0])
    left, middle, right = (blocks[i : i + 4] for i in (0, 4, 8))
    for kz in range(4):
        zh, zl = at[2][kz] // 2, at[2][kz] & 1
        block = pl.ds(4 * zh, 4)
        last = BLOCK - 2 * PART
        copy(
            right[kz].at[:, :, :, pl.ds(0, last)],
            xs.at[block, :, zl, :, pl.ds(2 * PART, last)],
            xsems.at[zh],
        )
        for k in range(4):
            copy(
                left[k].at[kz, :, :, pl.ds(0, PART)],
                xs.at[block, k, zl, :, pl.ds(0, PART)],
                xsems.at[zh],
            )
            copy(
                middle[k].at[:, kz],
                xs.at[4 * zh + k, :, zl, :, pl.ds(PART, PART)],
                xsems.at[zh],
            )
            columns = pl.ds(pl.multiple_of((2 * at[0][k] + zl) * 128, 128), 128)
            for part in range(2):
                copy(
                    right[kz].at[:, k, :, pl.ds(last + part * 128, 128)],
                    ws.at[block, pl.ds(4 * ROWS + part * RANK, RANK), columns],
                    bsems.at[zh],
                )
    for k in range(4):
        for kz in (0, 1 + core):
            zl = place[3] & 1 if isinstance(kz, int) else 1 - (place[3] & 1)
            columns = pl.ds(pl.multiple_of((2 * at[0][k] + zl) * 128, 128), 128)
            copy(left[k].at[kz, 0, :, pl.ds(PART, 128)], factor.at[:, columns], fsem)
    for j in range(1, NB):
        weights(*steps[j])

    for j, (zh, ky) in enumerate(steps):
        block = 4 * zh + ky
        if j % 4 == 0:
            await_all(xs.at[pl.ds(4 * zh, 4)], xsems.at[zh])
            await_all(ws.at[pl.ds(4 * zh, 4), pl.ds(4 * ROWS, 2 * RANK)], bsems.at[zh])
        await_all(ws.at[block, pl.ds(0, 4 * ROWS)], wsems.at[block])
        product = dot_t(ws[block], xs[block].reshape(TOK, BLOCK))
        if j == 0:
            acc[...] = product
        else:
            acc[...] += product
    t = acc[4 * ROWS :].astype(jnp.bfloat16)
    for side, a in enumerate((a_mine, a_other)):
        for k in range(2):
            low = jnp.dot(a[k], t[k * RANK : (k + 1) * RANK], preferred_element_type=jnp.float32)
            rows = (2 * side + k) * ROWS
            out[side, k] = (acc[rows : rows + ROWS] + low).astype(jnp.bfloat16)
    await_all(factor, fsem)


ANY = pl.BlockSpec(memory_space=pl.ANY)
ON_CHIP = pl.BlockSpec(memory_space=pltpu.VMEM)
SCALARS = pl.BlockSpec(memory_space=pltpu.SMEM)


def up(place, weights, others, a_mine, a_other, blocks):
    return pl.pallas_call(
        up_kernel,
        out_shape=[
            jax.ShapeDtypeStruct((2, 2, ROWS, TOK), jnp.bfloat16),
            jax.ShapeDtypeStruct((RANK, BLOCK), jnp.bfloat16),
        ],
        in_specs=[SCALARS, ANY, ANY, ON_CHIP, ON_CHIP, *[ANY] * 12],
        out_specs=[ON_CHIP, ON_CHIP],
        scratch_shapes=[
            pltpu.VMEM((NB, 4 * ROWS + 2 * RANK, BLOCK), jnp.bfloat16),
            pltpu.VMEM((NB, 4, 2, GROUP, BLOCK), jnp.bfloat16),
            pltpu.VMEM((4 * ROWS + 2 * RANK, TOK), jnp.float32),
            pltpu.SemaphoreType.DMA((NB,)),
            pltpu.SemaphoreType.DMA((2,)),
            pltpu.SemaphoreType.DMA((2,)),
            pltpu.SemaphoreType.DMA,
        ],
        compiler_params=pltpu.CompilerParams(vmem_limit_bytes=VMEM),
        name="up",
    )(place, weights, others, a_mine, a_other, *blocks)


def down_kernel(place, mine, other, w, wo, a_mine, a_other, *refs):
    outs, (ws, hidden, ob, wsems, osems) = refs[:12], refs[12:]
    core = place[0]
    for j in range(NB):
        there = 2 * (4 * (j // 4) + coordinate(place[2], j % 4, core)) + core
        columns = pl.ds(pl.multiple_of(there * BLOCK, BLOCK), BLOCK)
        for side, source in enumerate((w, wo)):
            copy(source.at[2, :, columns], ws.at[j, pl.ds(side * ROWS, ROWS)], wsems.at[j])
    f32 = jnp.float32

    def both(side, k):
        theirs = [other[1 - side, k, :, i * 128 : (i + 1) * 128] for i in (0, 2, 1, 3)]
        return mine[side, k].astype(f32) + jnp.concatenate(theirs, axis=1).astype(f32)

    halves = []
    for side in range(2):
        gate, upper = both(side, 0), both(side, 1)
        halves.append(gate / (1.0 + jnp.exp(-gate)) * upper)
    hidden[...] = jnp.concatenate(halves, axis=0).T.astype(jnp.bfloat16)
    factor = jnp.concatenate([a_mine[2], a_other[2]], axis=0)
    low = jnp.dot(hidden[...], factor, preferred_element_type=f32)
    low = jnp.concatenate([low, jnp.zeros_like(low)], axis=1).astype(jnp.bfloat16)
    rel_z = [relative(place[3], z, core) for z in range(4)]
    left, middle, right = (outs[i : i + 4] for i in (0, 4, 8))
    for j in range(NB):
        zh, ky = j // 4, j % 4
        await_all(ws.at[j], wsems.at[j])
        value = jnp.dot(hidden[...], ws[j], preferred_element_type=f32).astype(jnp.bfloat16)
        ob[j, :, :, :, :BLOCK] = value.reshape(4, 2, GROUP, BLOCK)
        ob[j, :, :, :, BLOCK:] = low.reshape(4, 2, GROUP, 128)
        for zl in range(2):
            kz = rel_z[2 * zh + zl]
            for kx in range(4):
                copy(
                    ob.at[j, kx, zl, :, pl.ds(0, PART)],
                    left[kx].at[kz, ky],
                    osems.at[j],
                )
            copy(
                ob.at[j, :, zl, :, pl.ds(PART, PART)],
                middle[ky].at[:, kz],
                osems.at[j],
            )
            for k in range(4):

                @pl.when(kz == k)
                def _():
                    copy(
                        ob.at[j, :, zl, :, pl.ds(2 * PART, PART)],
                        right[k].at[ky],
                        osems.at[j],
                    )
    for j in range(NB):
        await_all(ob.at[j], osems.at[j])


def down(place, mine, other, weights, others, a_mine, a_other):
    return pl.pallas_call(
        down_kernel,
        out_shape=[jax.ShapeDtypeStruct((4, 4, GROUP, PART), jnp.bfloat16)] * 12,
        in_specs=[SCALARS, ON_CHIP, ON_CHIP, ANY, ANY, ON_CHIP, ON_CHIP],
        out_specs=[ANY] * 12,
        scratch_shapes=[
            pltpu.VMEM((NB, 2 * ROWS, BLOCK), jnp.bfloat16),
            pltpu.VMEM((TOK, 2 * ROWS), jnp.bfloat16),
            pltpu.VMEM((NB, 4, 2, GROUP, WIDE), jnp.bfloat16),
            *[pltpu.SemaphoreType.DMA((NB,))] * 2,
        ],
        compiler_params=pltpu.CompilerParams(vmem_limit_bytes=VMEM),
        name="down",
    )(place, mine, other, weights, others, a_mine, a_other)


def per_device(tokens, frozen_weights, hidden_adapter_factor, feature_adapter_factor):
    zh, y, core, x, zl = (lax.axis_index(n) for n in NAMES)
    place = jnp.stack([core, x, y, 2 * zh + zl]).astype(jnp.int32)
    others = send(frozen_weights, CORES)
    a_other = send(hidden_adapter_factor, CORES)
    gate_factor, up_factor, down_factor = feature_adapter_factor
    blocks, (others, a_other) = gather([
        jnp.concatenate([tokens[:, :PART], down_factor], axis=1)[None],
        tokens[None, :, PART : 2 * PART],
        jnp.concatenate([tokens[:, 2 * PART :], gate_factor, up_factor], axis=1)[None],
    ], (others, a_other))
    blocks = [v.reshape(4, 4, *v.shape[1:]) for v in blocks]
    mine, factor = up(place, frozen_weights, others, hidden_adapter_factor, a_other, blocks)
    theirs = send(mine, CORES)
    sums = down(place, mine, theirs, frozen_weights, others, hidden_adapter_factor, a_other)
    left, middle, right = scatter(sums)
    last = BLOCK - 2 * PART
    plain = jnp.concatenate([left, middle, right[:, :last]], axis=1).astype(jnp.float32)
    extra = jnp.dot(
        right[:, last : last + RANK], factor, preferred_element_type=jnp.float32
    )
    return (plain + extra).astype(jnp.bfloat16)


def solution(mesh):
    fine = Mesh(mesh.devices.reshape(SIZES), NAMES)
    units = ("zh", "y", "c", "x", "zl")
    return jax.shard_map(
        per_device,
        mesh=fine,
        in_specs=(
            P(("x", "zl"), ("zh", "y", "c")),
            P(None, units, None),
            P(None, units, None),
            P(None, None, units),
        ),
        out_specs=P(("x", "zl"), ("zh", "y", "c")),
        check_vma=False,
    )
```

```python
import jax
import jax.numpy as jnp
from jax import lax
from jax.experimental import pallas as pl
from jax.experimental.pallas import tpu as pltpu
from jax.sharding import Mesh, PartitionSpec as P

NAMES = ("zh", "y", "c", "x", "zl")
SIZES = (2, 4, 2, 4, 2)
ROWS = 208
TOK = 512
GROUP = 64
BLOCK = 1024
NB = 8
RANK = 64
WIDE = BLOCK + 128
PART = WIDE // 3
ORDERS = ((1, 2, 0), (2, 0, 1), (0, 1, 2))
VMEM = 60 * 1024 * 1024


def pairs(move):
    out = []
    for i in range(128):
        zh, y, c, x, zl = i // 64, i // 16 % 4, i // 8 % 2, i // 2 % 4, i % 2
        x, y, z, c = move(x, y, 2 * zh + zl, c)
        out.append((i, (((z // 2 * 4 + y) * 2 + c) * 4 + x) * 2 + z % 2))
    return out


def axis_pairs(axis, first):
    def move(x, y, z, c):
        q = [x, y, z]
        q[axis] ^= 1 if (c == 0) == first else 3
        return (*q, c)

    return pairs(move)


FIRST = [axis_pairs(a, True) for a in range(3)]
SECOND = [axis_pairs(a, False) for a in range(3)]


CORES = pairs(lambda x, y, z, c: (x, y, z, 1 - c))


def send(value, table):
    return lax.ppermute(value, NAMES, table)


def gather(values, late):
    for stage in range(2):
        axes = [order[stage] for order in ORDERS]
        mine = [jnp.stack([v, send(v, FIRST[a])]) for v, a in zip(values, axes)]
        theirs = [send(v, SECOND[a]) for v, a in zip(mine, axes)]
        values = [
            jnp.concatenate(p).reshape(-1, *v.shape[1:])
            for p, v in zip(zip(mine, theirs), values)
        ]
        if stage == 1:
            values[1], late = lax.optimization_barrier((values[1], late))
    axes = [order[2] for order in ORDERS]
    turns = (2, 0, 1)
    near = {p: send(values[p], FIRST[axes[p]]) for p in turns}
    second = {p: send(values[p], SECOND[axes[p]]) for p in turns}
    across = {p: send(near[p], SECOND[axes[p]]) for p in turns}
    out = [b for p in range(3) for b in (values[p], near[p], second[p], across[p])]
    return out, late


def scatter(sums):
    totals = []
    for part, order in enumerate(ORDERS):
        blocks = [v.reshape(16, GROUP, PART) for v in sums[4 * part : 4 * part + 4]]
        across = blocks[1] + send(blocks[3], SECOND[order[2]])
        second = send(blocks[2], SECOND[order[2]])
        first = send(across, FIRST[order[2]])
        total = sum(v.astype(jnp.float32) for v in (blocks[0], second, first))
        totals.append(total.astype(jnp.bfloat16))
    for stage in (1, 0):
        axes = [order[stage] for order in ORDERS]
        keep, away = zip(*(t.reshape(2, 2, -1, GROUP, PART) for t in totals))
        halves = [k + send(w, SECOND[a]) for k, w, a in zip(keep, away, axes)]
        totals = [p[0] + send(p[1], FIRST[a]) for p, a in zip(halves, axes)]
    return [t.reshape(GROUP, PART) for t in totals]


def coordinate(place, k, core):
    return place ^ jnp.where(core == 0, (0, 1, 3, 2)[k], (0, 3, 1, 2)[k])


def relative(place, there, core):
    e = place ^ there
    zero = jnp.where(e == 1, 1, jnp.where(e == 3, 2, jnp.where(e == 2, 3, 0)))
    one = jnp.where(e == 3, 1, jnp.where(e == 1, 2, jnp.where(e == 2, 3, 0)))
    return jnp.where(core == 0, zero, one)


def dot_t(a, b):
    return lax.dot_general(a, b, (((1,), (1,)), ((), ())), preferred_element_type=jnp.float32)


def copy(source, target, sem):
    pltpu.make_async_copy(source, target, sem).start()


def await_all(target, sem):
    pltpu.make_async_copy(target, target, sem).wait()


def up_kernel(place, w, wo, a_mine, a_other, *refs):
    blocks, (out, factor, ws, xs, acc, wsems, xsems, bsems, fsem) = refs[:12], refs[12:]
    core = place[0]
    at = [[coordinate(place[1 + a], k, core) for k in range(4)] for a in range(3)]
    near = place[3] // 2
    steps = [(near if j < 4 else 1 - near, j % 4) for j in range(NB)]

    def weights(zh, ky):
        columns = pl.ds(pl.multiple_of((2 * (4 * zh + at[1][ky]) + core) * BLOCK, BLOCK), BLOCK)
        block = 4 * zh + ky
        for side, source in enumerate((w, wo)):
            for k in range(2):
                rows = pl.ds((2 * side + k) * ROWS, ROWS)
                copy(source.at[k, :, columns], ws.at[block, rows], wsems.at[block])

    weights(*steps[0])
    left, middle, right = (blocks[i : i + 4] for i in (0, 4, 8))
    for kz in range(4):
        zh, zl = at[2][kz] // 2, at[2][kz] & 1
        block = pl.ds(4 * zh, 4)
        last = BLOCK - 2 * PART
        copy(
            right[kz].at[:, :, :, pl.ds(0, last)],
            xs.at[block, :, zl, :, pl.ds(2 * PART, last)],
            xsems.at[zh],
        )
        for k in range(4):
            copy(
                left[k].at[kz, :, :, pl.ds(0, PART)],
                xs.at[block, k, zl, :, pl.ds(0, PART)],
                xsems.at[zh],
            )
            copy(
                middle[k].at[:, kz],
                xs.at[4 * zh + k, :, zl, :, pl.ds(PART, PART)],
                xsems.at[zh],
            )
            columns = pl.ds(pl.multiple_of((2 * at[0][k] + zl) * 128, 128), 128)
            for part in range(2):
                copy(
                    right[kz].at[:, k, :, pl.ds(last + part * 128, 128)],
                    ws.at[block, pl.ds(4 * ROWS + part * RANK, RANK), columns],
                    bsems.at[zh],
                )
    for k in range(4):
        for kz in (0, 1 + core):
            zl = place[3] & 1 if isinstance(kz, int) else 1 - (place[3] & 1)
            columns = pl.ds(pl.multiple_of((2 * at[0][k] + zl) * 128, 128), 128)
            copy(left[k].at[kz, 0, :, pl.ds(PART, 128)], factor.at[:, columns], fsem)
    for j in range(1, NB):
        weights(*steps[j])

    for j, (zh, ky) in enumerate(steps):
        block = 4 * zh + ky
        if j % 4 == 0:
            await_all(xs.at[pl.ds(4 * zh, 4)], xsems.at[zh])
            await_all(ws.at[pl.ds(4 * zh, 4), pl.ds(4 * ROWS, 2 * RANK)], bsems.at[zh])
        await_all(ws.at[block, pl.ds(0, 4 * ROWS)], wsems.at[block])
        product = dot_t(ws[block], xs[block].reshape(TOK, BLOCK))
        if j == 0:
            acc[...] = product
        else:
            acc[...] += product
    t = acc[4 * ROWS :].astype(jnp.bfloat16)
    for side, a in enumerate((a_mine, a_other)):
        for k in range(2):
            low = jnp.dot(a[k], t[k * RANK : (k + 1) * RANK], preferred_element_type=jnp.float32)
            rows = (2 * side + k) * ROWS
            out[side, k] = (acc[rows : rows + ROWS] + low).astype(jnp.bfloat16)
    await_all(factor, fsem)


ANY = pl.BlockSpec(memory_space=pl.ANY)
ON_CHIP = pl.BlockSpec(memory_space=pltpu.VMEM)
SCALARS = pl.BlockSpec(memory_space=pltpu.SMEM)


def up(place, weights, others, a_mine, a_other, blocks):
    return pl.pallas_call(
        up_kernel,
        out_shape=[
            jax.ShapeDtypeStruct((2, 2, ROWS, TOK), jnp.bfloat16),
            jax.ShapeDtypeStruct((RANK, BLOCK), jnp.bfloat16),
        ],
        in_specs=[SCALARS, ANY, ANY, ON_CHIP, ON_CHIP, *[ANY] * 12],
        out_specs=[ON_CHIP, ON_CHIP],
        scratch_shapes=[
            pltpu.VMEM((NB, 4 * ROWS + 2 * RANK, BLOCK), jnp.bfloat16),
            pltpu.VMEM((NB, 4, 2, GROUP, BLOCK), jnp.bfloat16),
            pltpu.VMEM((4 * ROWS + 2 * RANK, TOK), jnp.float32),
            pltpu.SemaphoreType.DMA((NB,)),
            pltpu.SemaphoreType.DMA((2,)),
            pltpu.SemaphoreType.DMA((2,)),
            pltpu.SemaphoreType.DMA,
        ],
        compiler_params=pltpu.CompilerParams(vmem_limit_bytes=VMEM),
        name="up",
    )(place, weights, others, a_mine, a_other, *blocks)


def down_kernel(place, mine, other, w, wo, a_mine, a_other, *refs):
    outs, (ws, hidden, ob, wsems, osems) = refs[:12], refs[12:]
    core = place[0]
    for j in range(NB):
        there = 2 * (4 * (j // 4) + coordinate(place[2], j % 4, core)) + core
        columns = pl.ds(pl.multiple_of(there * BLOCK, BLOCK), BLOCK)
        for side, source in enumerate((w, wo)):
            copy(source.at[2, :, columns], ws.at[j, pl.ds(side * ROWS, ROWS)], wsems.at[j])
    f32 = jnp.float32

    def both(side, k):
        theirs = [other[1 - side, k, :, i * 128 : (i + 1) * 128] for i in (0, 2, 1, 3)]
        return mine[side, k].astype(f32) + jnp.concatenate(theirs, axis=1).astype(f32)

    halves = []
    for side in range(2):
        gate, upper = both(side, 0), both(side, 1)
        halves.append(gate / (1.0 + jnp.exp(-gate)) * upper)
    hidden[...] = jnp.concatenate(halves, axis=0).T.astype(jnp.bfloat16)
    factor = jnp.concatenate([a_mine[2], a_other[2]], axis=0)
    low = jnp.dot(hidden[...], factor, preferred_element_type=f32)
    low = jnp.concatenate([low, jnp.zeros_like(low)], axis=1).astype(jnp.bfloat16)
    rel_z = [relative(place[3], z, core) for z in range(4)]
    left, middle, right = (outs[i : i + 4] for i in (0, 4, 8))
    for j in range(NB):
        zh, ky = j // 4, j % 4
        await_all(ws.at[j], wsems.at[j])
        value = jnp.dot(hidden[...], ws[j], preferred_element_type=f32).astype(jnp.bfloat16)
        ob[j, :, :, :, :BLOCK] = value.reshape(4, 2, GROUP, BLOCK)
        ob[j, :, :, :, BLOCK:] = low.reshape(4, 2, GROUP, 128)
        for zl in range(2):
            kz = rel_z[2 * zh + zl]
            for kx in range(4):
                copy(
                    ob.at[j, kx, zl, :, pl.ds(0, PART)],
                    left[kx].at[kz, ky],
                    osems.at[j],
                )
            copy(
                ob.at[j, :, zl, :, pl.ds(PART, PART)],
                middle[ky].at[:, kz],
                osems.at[j],
            )
            for k in range(4):

                @pl.when(kz == k)
                def _():
                    copy(
                        ob.at[j, :, zl, :, pl.ds(2 * PART, PART)],
                        right[k].at[ky],
                        osems.at[j],
                    )
    for j in range(NB):
        await_all(ob.at[j], osems.at[j])


def down(place, mine, other, weights, others, a_mine, a_other):
    return pl.pallas_call(
        down_kernel,
        out_shape=[jax.ShapeDtypeStruct((4, 4, GROUP, PART), jnp.bfloat16)] * 12,
        in_specs=[SCALARS, ON_CHIP, ON_CHIP, ANY, ANY, ON_CHIP, ON_CHIP],
        out_specs=[ANY] * 12,
        scratch_shapes=[
            pltpu.VMEM((NB, 2 * ROWS, BLOCK), jnp.bfloat16),
            pltpu.VMEM((TOK, 2 * ROWS), jnp.bfloat16),
            pltpu.VMEM((NB, 4, 2, GROUP, WIDE), jnp.bfloat16),
            *[pltpu.SemaphoreType.DMA((NB,))] * 2,
        ],
        compiler_params=pltpu.CompilerParams(vmem_limit_bytes=VMEM),
        name="down",
    )(place, mine, other, weights, others, a_mine, a_other)


def per_device(tokens, frozen_weights, hidden_adapter_factor, feature_adapter_factor):
    zh, y, core, x, zl = (lax.axis_index(n) for n in NAMES)
    place = jnp.stack([core, x, y, 2 * zh + zl]).astype(jnp.int32)
    others = send(frozen_weights, CORES)
    a_other = send(hidden_adapter_factor, CORES)
    gate_factor, up_factor, down_factor = feature_adapter_factor
    blocks, (others, a_other) = gather([
        jnp.concatenate([tokens[:, :PART], down_factor], axis=1)[None],
        tokens[None, :, PART : 2 * PART],
        jnp.concatenate([tokens[:, 2 * PART :], gate_factor, up_factor], axis=1)[None],
    ], (others, a_other))
    blocks = [v.reshape(4, 4, *v.shape[1:]) for v in blocks]
    mine, factor = up(place, frozen_weights, others, hidden_adapter_factor, a_other, blocks)
    theirs = send(mine, CORES)
    sums = down(place, mine, theirs, frozen_weights, others, hidden_adapter_factor, a_other)
    left, middle, right = scatter(sums)
    last = BLOCK - 2 * PART
    plain = jnp.concatenate([left, middle, right[:, :last]], axis=1).astype(jnp.float32)
    extra = jnp.dot(
        right[:, last : last + RANK], factor, preferred_element_type=jnp.float32
    )
    return (plain + extra).astype(jnp.bfloat16)


def solution(mesh):
    fine = Mesh(mesh.devices.reshape(SIZES), NAMES)
    units = ("zh", "y", "c", "x", "zl")
    return jax.shard_map(
        per_device,
        mesh=fine,
        in_specs=(
            P(("x", "zl"), ("zh", "y", "c")),
            P(None, units, None),
            P(None, units, None),
            P(None, None, units),
        ),
        out_specs=P(("x", "zl"), ("zh", "y", "c")),
        check_vma=False,
    )
```
